32 devices in a mesh: brick: 8 (over z, y), stack: 4 (over x, core).
Axes of the slice: x: 2, y: 2, z: 4, core: 2. Of those that a mesh axis runs over, the one named last changes fastest.
Arguments:
- estimate: float32 [64, 256, 128], P('stack', 'brick'), may hold values from 0.5 to 2
- view_data: float32 [6, 64, 256, 128], P(None, 'stack', 'brick'), may hold values from 0.25 to 4
- psf_taps: float32 [6, 3, 31], replicated, may hold values from 0.05 to 1
- offsets: int32 [6], replicated, may hold values from 0 to 7, as said below
- coverage: int32 [6, 8], P(None, 'brick'), may hold values from 0 to 1, as said below
Outputs:
- updated: float32 [64, 256, 128], P('stack', 'brick')
The draws below stay inside these ranges and needn't reach their ends.
Inputs may be any that keep to these rules, and one draw needn't show every extreme that they name: Tile j of view v images brick (j + offsets[v]) mod 8. `coverage`: every brick is covered by at least one view.
All inputs are finite; a program needn't handle non-finite values.
Results may differ from the reference program's by a relative error of at most 0.0001.
Values sent between devices are 32-bit elements; how exact they have to be, the bound alone decides.
A program may use at most 128 MiB of HBM per device.

```python
import math
import jax
import jax.numpy as jnp
from jax import lax

V = 6
TAPS = 31
HALF = 15
X = 128
CY = 32
NZ = 64
NY = 256
TILES = 8


def draw_offsets(key, part):
    first_key = jax.random.fold_in(key, 11)
    second_key = jax.random.fold_in(key, 12)
    values = jax.random.randint(first_key, (V,), 0, TILES)
    view_order = jax.random.permutation(second_key, V)
    bit_count = (TILES - 1).bit_length()
    for bit_index in range(bit_count):
        target = view_order[bit_index]
        values = values.at[target].set(jnp.bitwise_or(values[target], 1 << bit_index))
    values = values.at[view_order[bit_count]].set(TILES - 1)
    return values.astype(jnp.int32)


def draw_coverage(key, part):
    first_key = jax.random.fold_in(key, 21)
    second_key = jax.random.fold_in(key, 22)
    chance = jax.random.randint(first_key, (V, TILES), 0, 100)
    forced = jax.random.randint(second_key, (TILES,), 0, V)
    picked = jnp.arange(V)[:, None] == forced[None, :]
    return jnp.logical_or(chance < 55, picked).astype(jnp.int32)


def steps_of(key, shape, cuts, low, high):
    factor_of, own = 1.0, jax.random.fold_in(key, 6)
    for position, blocks in cuts:
        heights = jnp.exp(jax.random.uniform(jax.random.fold_in(own, position), (blocks,), jnp.float32, low / len(cuts), high / len(cuts)))
        factor_of = factor_of * jnp.repeat(heights, shape[position] // blocks).reshape([-1 if axis == position else 1 for axis in range(len(shape))])
    return factor_of


def setup_inputs(seed: int = 0) -> dict:
    key_of = jax.random.split(jax.random.key(seed), 6)
    estimate = jnp.clip(0.5 + 1.5 * jax.random.uniform(key_of[0], (NZ, NY, X), jnp.float32) ** steps_of(key_of[0], (NZ, NY, X), ((0, 4), (1, 8)), -0.2, 0.2), 0.5, 2.0)
    view_data = jnp.clip(jnp.exp(math.log(4.0) - 2.7725887 * jax.random.uniform(key_of[1], (V, NZ, NY, X), jnp.float32) ** steps_of(key_of[1], (V, NZ, NY, X), ((1, 4), (2, 8)), -0.2, 0.2)), 0.25, 4.0)
    psf_taps = jnp.clip(jnp.exp(jax.random.uniform(key_of[2], (V, 3, TAPS), jnp.float32, math.log(0.05), math.log(1.0))), 0.05, 1.0)
    offsets = draw_offsets(jax.random.fold_in(key_of[5], 71), 0)
    coverage = draw_coverage(jax.random.fold_in(key_of[5], 71), 0)
    return dict(estimate=estimate, view_data=view_data, psf_taps=psf_taps, offsets=offsets, coverage=coverage)


def band_matrix(taps, out_count, in_count, lead):
    out_index = jnp.arange(out_count)[:, None]
    in_index = jnp.arange(in_count)[None, :]
    distance = in_index - out_index + lead
    matrix = jnp.zeros((out_count, in_count), jnp.float32)
    for tap_index in range(TAPS):
        matrix = matrix + jnp.where(distance == tap_index, taps[tap_index], jnp.float32(0.0))
    return matrix


def along_first(matrix, field):
    return jnp.einsum("ij,jyx->iyx", matrix, field, precision=lax.Precision.HIGHEST)


def along_second(matrix, field):
    return jnp.einsum("ij,zjx->zix", matrix, field, precision=lax.Precision.HIGHEST)


def along_third(matrix, field):
    return jnp.einsum("ij,zyj->zyi", matrix, field, precision=lax.Precision.HIGHEST)


def reference(estimate, view_data, psf_taps, offsets, coverage):
    kernels = psf_taps / jnp.sum(psf_taps, axis=-1, keepdims=True)
    flipped = kernels[..., ::-1]
    cover_count = jnp.repeat(jnp.sum(coverage, axis=0), CY).astype(jnp.float32)
    summed = jnp.zeros_like(estimate)
    for view_index in range(V):
        blurred = along_first(band_matrix(kernels[view_index, 0], NZ, NZ, HALF), estimate)
        blurred = along_second(band_matrix(kernels[view_index, 1], NY, NY, HALF), blurred)
        blurred = along_third(band_matrix(kernels[view_index, 2], X, X, HALF), blurred)
        recorded = view_data[view_index].astype(jnp.float32)
        doubled = jnp.concatenate([recorded, recorded], axis=1)
        start_row = (NY - offsets[view_index] * CY).astype(jnp.int32)
        owned_data = lax.dynamic_slice_in_dim(doubled, start_row, NY, axis=1)
        cover_mask = jnp.repeat(coverage[view_index], CY).astype(jnp.float32)
        ratio_field = cover_mask[None, :, None] * owned_data / blurred
        back_field = along_third(band_matrix(flipped[view_index, 2], X, X, HALF), ratio_field)
        back_field = along_second(band_matrix(flipped[view_index, 1], NY, NY, HALF), back_field)
        back_field = along_first(band_matrix(flipped[view_index, 0], NZ, NZ, HALF), back_field)
        summed = summed + back_field
    return estimate * summed / cover_count[None, :, None]
```

```python
import functools

import jax
import jax.numpy as jnp
from jax import lax
from jax.experimental import pallas as pl
from jax.experimental.pallas import tpu as pltpu
from jax.sharding import PartitionSpec as P

VIEWS = 6
TAPS = 31
HALF = 15
WIDTH = 128
ROWS = 32
DEPTH = 16
PAD = 16
EROWS = ROWS + 2 * PAD
EDEPTH = DEPTH + 2 * PAD
F32 = jnp.float32
BF16 = jnp.bfloat16


def split(x):
    hi = x.astype(BF16)
    lo = (x - hi.astype(F32)).astype(BF16)
    return hi, lo


def iota(shape, dim):
    return lax.broadcasted_iota(jnp.int32, shape, dim)


def spread_taps(distance, taps_ref, view, dim):
    total = jnp.float32(0.0)
    matrix = jnp.zeros(distance.shape, F32)
    for tap in range(TAPS):
        value = taps_ref[view, dim, tap]
        total = total + value
        matrix = jnp.where(distance == tap, value, matrix)
    return matrix / total


def hi_hi_lo(matrix, part):
    hi, lo = split(matrix)
    return jnp.where(part < 2, hi.astype(F32), lo.astype(F32)).astype(BF16)


def build_forward(taps_ref, wz_ref, wy_ref, wx_ref):
    def one(view, carry):
        col = iota((DEPTH, 3 * EDEPTH), 1)
        dist = col % EDEPTH - iota((DEPTH, 3 * EDEPTH), 0) - 1
        wz_ref[pl.ds(pl.multiple_of(view * DEPTH, DEPTH), DEPTH), :] = hi_hi_lo(
            spread_taps(dist, taps_ref, view, 0), col // EDEPTH
        )
        col = iota((ROWS, 3 * EROWS), 1)
        dist = col % EROWS - iota((ROWS, 3 * EROWS), 0) - 1
        wy_ref[view] = hi_hi_lo(spread_taps(dist, taps_ref, view, 1), col // EROWS)
        dist = iota((WIDTH, WIDTH), 0) - iota((WIDTH, WIDTH), 1) + HALF
        hi, lo = split(spread_taps(dist, taps_ref, view, 2))
        wx_ref[view, 0:WIDTH] = hi
        wx_ref[view, WIDTH : 2 * WIDTH] = hi
        wx_ref[view, 2 * WIDTH : 3 * WIDTH] = lo
        return carry

    lax.fori_loop(0, VIEWS, one, 0)


def build_backward(taps_ref, wz_ref, wy_ref, wx_ref, wide_ref):
    wide_ref[...] = jnp.zeros_like(wide_ref)

    def one(view, carry):
        col = iota(wide_ref.shape, 1)
        inner = col % (VIEWS * DEPTH) - view * DEPTH
        dist = iota(wide_ref.shape, 0) - inner - 1
        dist = jnp.where((inner >= 0) & (inner < DEPTH), dist, -1)
        wide_ref[...] += spread_taps(dist, taps_ref, view, 0)
        col = iota((EROWS, 3 * ROWS), 1)
        dist = iota((EROWS, 3 * ROWS), 0) - col % ROWS - 1
        wy_ref[view] = hi_hi_lo(spread_taps(dist, taps_ref, view, 1), col // ROWS)
        dist = iota((WIDTH, WIDTH), 1) - iota((WIDTH, WIDTH), 0) + HALF
        hi, lo = split(spread_taps(dist, taps_ref, view, 2))
        wx_ref[view, 0:WIDTH] = hi
        wx_ref[view, WIDTH : 2 * WIDTH] = hi
        wx_ref[view, 2 * WIDTH : 3 * WIDTH] = lo
        return carry

    lax.fori_loop(0, VIEWS, one, 0)
    wz_ref[...] = hi_hi_lo(wide_ref[...], iota(wide_ref.shape, 1) // (VIEWS * DEPTH))


def stacked(x, axis):
    hi, lo = split(x)
    return jnp.concatenate([hi, lo, hi], axis=axis)


def dot(a, b):
    return jnp.dot(a, b, preferred_element_type=F32)


def axial_forward(ext_ref, wz_ref, axial_ref):
    def one(step, carry):
        for inner in range(2):
            y = step * 4 + inner * 2
            field = jnp.concatenate(
                [ext_ref[pl.ds(y + k, EDEPTH, stride=EROWS), :] for k in range(2)], axis=1
            )
            out = dot(wz_ref[...], stacked(field, 0))
            for k in range(2):
                axial_ref[pl.ds(y + k, VIEWS * DEPTH, stride=EROWS), :] = out[
                    :, k * WIDTH : (k + 1) * WIDTH
                ]
        return carry

    lax.fori_loop(0, EROWS // 4, one, 0)


def lateral_forward(view, axial_ref, wy_ref, side_ref):
    for z in range(0, DEPTH, 2):
        base = (view * DEPTH + z) * EROWS
        field = jnp.concatenate(
            [
                axial_ref[pl.ds(pl.multiple_of(base + k * EROWS, EROWS), EROWS), :]
                for k in range(2)
            ],
            axis=1,
        )
        out = dot(wy_ref[view], stacked(field, 0))
        for k in range(2):
            side_ref[(z + k) * ROWS : (z + k + 1) * ROWS, :] = out[
                :, k * WIDTH : (k + 1) * WIDTH
            ]


def lateral_backward(view, side_ref, wy_ref, back_ref):
    for z in range(0, DEPTH, 2):
        field = jnp.concatenate(
            [side_ref[(z + k) * ROWS : (z + k + 1) * ROWS, :] for k in range(2)], axis=1
        )
        out = dot(wy_ref[view], stacked(field, 0))
        base = (view * DEPTH + z) * EROWS
        for k in range(2):
            back_ref[pl.ds(pl.multiple_of(base + k * EROWS, EROWS), EROWS), :] = out[
                :, k * WIDTH : (k + 1) * WIDTH
            ]


def axial_backward(back_ref, wz_ref, out_ref):
    def one(step, carry):
        for inner in range(2):
            y = step * 4 + inner * 2
            field = jnp.concatenate(
                [
                    back_ref[pl.ds(y + k, VIEWS * DEPTH, stride=EROWS), :]
                    for k in range(2)
                ],
                axis=1,
            )
            out = dot(wz_ref[...], stacked(field, 0))
            for k in range(2):
                out_ref[pl.ds(y + k, EDEPTH, stride=EROWS), :] = out[
                    :, k * WIDTH : (k + 1) * WIDTH
                ]
        return carry

    lax.fori_loop(0, EROWS // 4, one, 0)


FORWARD_SCRATCH = [
    pltpu.VMEM((VIEWS * DEPTH, 3 * EDEPTH), BF16),
    pltpu.VMEM((VIEWS, ROWS, 3 * EROWS), BF16),
    pltpu.VMEM((VIEWS, 3 * WIDTH, WIDTH), BF16),
    pltpu.VMEM((VIEWS * DEPTH * EROWS, WIDTH), F32),
    pltpu.VMEM((DEPTH * ROWS, WIDTH), F32),
]
BACKWARD_SCRATCH = [
    pltpu.VMEM((EDEPTH, 3 * VIEWS * DEPTH), BF16),
    pltpu.VMEM((VIEWS, EROWS, 3 * ROWS), BF16),
    pltpu.VMEM((VIEWS, 3 * WIDTH, WIDTH), BF16),
    pltpu.VMEM((EDEPTH, 3 * VIEWS * DEPTH), F32),
    pltpu.VMEM((DEPTH * ROWS, WIDTH), F32),
    pltpu.VMEM((VIEWS * DEPTH * EROWS, WIDTH), F32),
]
VMEM = pl.BlockSpec(memory_space=pltpu.VMEM)
SMEM = pl.BlockSpec(memory_space=pltpu.SMEM)


def blur_kernel(taps_ref, ext_ref, blur_ref, wz, wy, wx, axial, side):
    build_forward(taps_ref, wz, wy, wx)
    axial_forward(ext_ref, wz, axial)

    def one(view, carry):
        lateral_forward(view, axial, wy, side)
        blur_ref[view] = dot(stacked(side[...], 1), wx[view])
        return carry

    lax.fori_loop(0, VIEWS, one, 0)


def back_kernel(taps_ref, cover_ref, tiles_ref, blur_ref, out_ref, wz, wy, wx, wide, side, back):
    build_backward(taps_ref, wz, wy, wx, wide)

    def one(view, carry):
        cover = cover_ref[view, 0].astype(F32)
        ratio = cover * tiles_ref[view] / blur_ref[view]
        side[...] = dot(stacked(ratio, 1), wx[view])
        lateral_backward(view, side, wy, back)
        return carry

    lax.fori_loop(0, VIEWS, one, 0)
    axial_backward(back, wz, out_ref)


def send(array, axis, by):
    count = lax.axis_size(axis)
    return lax.ppermute(
        array, axis, [(i, i + by) for i in range(count) if 0 <= i + by < count]
    )


def rotate(array, axis, by):
    count = lax.axis_size(axis)
    return lax.ppermute(array, axis, [(i, (i + by) % count) for i in range(count)])


def shards(estimate, view_data, psf_taps, offsets, coverage):
    bricks = lax.axis_size("brick")
    tiles = []
    for view in range(VIEWS):
        choices = [functools.partial(lambda t, by: rotate(t, "brick", by), by=k) for k in range(1, bricks)]
        tiles.append(lax.switch(offsets[view], [lambda t: t] + choices, view_data[view]))
    tiles = jnp.stack(tiles).reshape(VIEWS, DEPTH * ROWS, WIDTH)
    wide = jnp.concatenate(
        [
            send(estimate[:, ROWS - PAD :], "brick", 1),
            estimate,
            send(estimate[:, :PAD], "brick", -1),
        ],
        axis=1,
    )
    ext = jnp.concatenate([send(wide, "stack", 1), wide, send(wide, "stack", -1)], axis=0)
    limit = pltpu.CompilerParams(vmem_limit_bytes=48 * 1024 * 1024)
    blur = pl.pallas_call(
        blur_kernel,
        out_shape=jax.ShapeDtypeStruct((VIEWS, DEPTH * ROWS, WIDTH), F32),
        in_specs=[SMEM, VMEM],
        out_specs=VMEM,
        scratch_shapes=FORWARD_SCRATCH,
        compiler_params=limit,
    )(psf_taps, ext.reshape(EDEPTH * EROWS, WIDTH))
    out = pl.pallas_call(
        back_kernel,
        out_shape=jax.ShapeDtypeStruct((EDEPTH * EROWS, WIDTH), F32),
        in_specs=[SMEM, SMEM, VMEM, VMEM],
        out_specs=VMEM,
        scratch_shapes=BACKWARD_SCRATCH,
        compiler_params=limit,
    )(psf_taps, coverage, tiles, blur)
    out = out.reshape(EDEPTH, EROWS, WIDTH)
    mid = (
        out[PAD : PAD + DEPTH]
        + send(out[:PAD], "stack", -1)
        + send(out[PAD + DEPTH :], "stack", 1)
    )
    low = send(mid[:, :PAD], "brick", -1)
    high = send(mid[:, PAD + ROWS :], "brick", 1)
    total = mid[:, PAD : PAD + ROWS] + jnp.concatenate([high, low], axis=1)
    count = jnp.sum(coverage[:, 0]).astype(F32)
    return estimate * total / count


def solution(mesh):
    placed = (
        P("stack", "brick", None),
        P(None, "stack", "brick", None),
        P(),
        P(),
        P(None, "brick"),
    )
    return jax.shard_map(
        shards, mesh=mesh, in_specs=placed, out_specs=P("stack", "brick", None), check_vma=False
    )
```

```python
import functools

import jax
import jax.numpy as jnp
from jax import lax
from jax.experimental import pallas as pl
from jax.experimental.pallas import tpu as pltpu
from jax.sharding import PartitionSpec as P

VIEWS = 6
TAPS = 31
HALF = 15
WIDTH = 128
ROWS = 32
DEPTH = 16
PAD = 16
EROWS = ROWS + 2 * PAD
EDEPTH = DEPTH + 2 * PAD
F32 = jnp.float32
BF16 = jnp.bfloat16


def split(x):
    hi = x.astype(BF16)
    lo = (x - hi.astype(F32)).astype(BF16)
    return hi, lo


def iota(shape, dim):
    return lax.broadcasted_iota(jnp.int32, shape, dim)


def spread_taps(distance, taps_ref, view, dim):
    total = jnp.float32(0.0)
    matrix = jnp.zeros(distance.shape, F32)
    for tap in range(TAPS):
        value = taps_ref[view, dim, tap]
        total = total + value
        matrix = jnp.where(distance == tap, value, matrix)
    return matrix / total


def hi_hi_lo(matrix, part):
    hi, lo = split(matrix)
    return jnp.where(part < 2, hi.astype(F32), lo.astype(F32)).astype(BF16)


def build_forward(taps_ref, wz_ref, wy_ref, wx_ref):
    def one(view, carry):
        col = iota((DEPTH, 3 * EDEPTH), 1)
        dist = col % EDEPTH - iota((DEPTH, 3 * EDEPTH), 0) - 1
        wz_ref[pl.ds(pl.multiple_of(view * DEPTH, DEPTH), DEPTH), :] = hi_hi_lo(
            spread_taps(dist, taps_ref, view, 0), col // EDEPTH
        )
        col = iota((ROWS, 3 * EROWS), 1)
        dist = col % EROWS - iota((ROWS, 3 * EROWS), 0) - 1
        wy_ref[view] = hi_hi_lo(spread_taps(dist, taps_ref, view, 1), col // EROWS)
        dist = iota((WIDTH, WIDTH), 0) - iota((WIDTH, WIDTH), 1) + HALF
        hi, lo = split(spread_taps(dist, taps_ref, view, 2))
        wx_ref[view, 0:WIDTH] = hi
        wx_ref[view, WIDTH : 2 * WIDTH] = hi
        wx_ref[view, 2 * WIDTH : 3 * WIDTH] = lo
        return carry

    lax.fori_loop(0, VIEWS, one, 0)


def build_backward(taps_ref, wz_ref, wy_ref, wx_ref, wide_ref):
    wide_ref[...] = jnp.zeros_like(wide_ref)

    def one(view, carry):
        col = iota(wide_ref.shape, 1)
        inner = col % (VIEWS * DEPTH) - view * DEPTH
        dist = iota(wide_ref.shape, 0) - inner - 1
        dist = jnp.where((inner >= 0) & (inner < DEPTH), dist, -1)
        wide_ref[...] += spread_taps(dist, taps_ref, view, 0)
        col = iota((EROWS, 3 * ROWS), 1)
        dist = iota((EROWS, 3 * ROWS), 0) - col % ROWS - 1
        wy_ref[view] = hi_hi_lo(spread_taps(dist, taps_ref, view, 1), col // ROWS)
        dist = iota((WIDTH, WIDTH), 1) - iota((WIDTH, WIDTH), 0) + HALF
        hi, lo = split(spread_taps(dist, taps_ref, view, 2))
        wx_ref[view, 0:WIDTH] = hi
        wx_ref[view, WIDTH : 2 * WIDTH] = hi
        wx_ref[view, 2 * WIDTH : 3 * WIDTH] = lo
        return carry

    lax.fori_loop(0, VIEWS, one, 0)
    wz_ref[...] = hi_hi_lo(wide_ref[...], iota(wide_ref.shape, 1) // (VIEWS * DEPTH))


def stacked(x, axis):
    hi, lo = split(x)
    return jnp.concatenate([hi, lo, hi], axis=axis)


def dot(a, b):
    return jnp.dot(a, b, preferred_element_type=F32)


def axial_forward(ext_ref, wz_ref, axial_ref):
    def one(step, carry):
        for inner in range(2):
            y = step * 4 + inner * 2
            field = jnp.concatenate(
                [ext_ref[pl.ds(y + k, EDEPTH, stride=EROWS), :] for k in range(2)], axis=1
            )
            out = dot(wz_ref[...], stacked(field, 0))
            for k in range(2):
                axial_ref[pl.ds(y + k, VIEWS * DEPTH, stride=EROWS), :] = out[
                    :, k * WIDTH : (k + 1) * WIDTH
                ]
        return carry

    lax.fori_loop(0, EROWS // 4, one, 0)


def lateral_forward(view, axial_ref, wy_ref, side_ref):
    for z in range(0, DEPTH, 2):
        base = (view * DEPTH + z) * EROWS
        field = jnp.concatenate(
            [
                axial_ref[pl.ds(pl.multiple_of(base + k * EROWS, EROWS), EROWS), :]
                for k in range(2)
            ],
            axis=1,
        )
        out = dot(wy_ref[view], stacked(field, 0))
        for k in range(2):
            side_ref[(z + k) * ROWS : (z + k + 1) * ROWS, :] = out[
                :, k * WIDTH : (k + 1) * WIDTH
            ]


def lateral_backward(view, side_ref, wy_ref, back_ref):
    for z in range(0, DEPTH, 2):
        field = jnp.concatenate(
            [side_ref[(z + k) * ROWS : (z + k + 1) * ROWS, :] for k in range(2)], axis=1
        )
        out = dot(wy_ref[view], stacked(field, 0))
        base = (view * DEPTH + z) * EROWS
        for k in range(2):
            back_ref[pl.ds(pl.multiple_of(base + k * EROWS, EROWS), EROWS), :] = out[
                :, k * WIDTH : (k + 1) * WIDTH
            ]


def axial_backward(back_ref, wz_ref, out_ref):
    def one(step, carry):
        for inner in range(2):
            y = step * 4 + inner * 2
            field = jnp.concatenate(
                [
                    back_ref[pl.ds(y + k, VIEWS * DEPTH, stride=EROWS), :]
                    for k in range(2)
                ],
                axis=1,
            )
            out = dot(wz_ref[...], stacked(field, 0))
            for k in range(2):
                out_ref[pl.ds(y + k, EDEPTH, stride=EROWS), :] = out[
                    :, k * WIDTH : (k + 1) * WIDTH
                ]
        return carry

    lax.fori_loop(0, EROWS // 4, one, 0)


CHUNK = 2
CHUNKS = VIEWS // CHUNK
CELLS = DEPTH * ROWS
SLAB = DEPTH * EROWS
EDGE = HALF * EROWS
ANY = pl.BlockSpec(memory_space=pl.ANY)
VMEM = pl.BlockSpec(memory_space=pltpu.VMEM)
SMEM = pl.BlockSpec(memory_space=pltpu.SMEM)


def kernel(
    bricks, stacks, taps_ref, offsets_ref, cover_ref, est_hbm, est_ref, view_ref, out_ref,
    mid0, mid1, mid2, stage, owned,
    halo, ext, wz, wy, wx, axial, side, blur,
    bz, by, bx, wide, back, spill, from_stack, to_brick, from_brick,
    send1, recv1, local1, send2, recv2, hsend, hrecv, ssend, srecv, tsend, trecv, usend, urecv,
):
    mids = (mid0, mid1, mid2)
    me = lax.axis_index("brick")
    level = lax.axis_index("stack")
    part = CELLS // bricks

    def to(axis, index, source, target, send_sem, recv_sem):
        return pltpu.make_async_remote_copy(
            src_ref=source,
            dst_ref=target,
            send_sem=send_sem,
            recv_sem=recv_sem,
            device_id={axis: index},
            device_id_type=pl.DeviceIdType.MESH,
        )

    def peer(step):
        return lax.rem(me + step, bricks)

    def rows(index):
        return pl.ds(pl.multiple_of(index * part, part), part)

    sides = (
        ("brick", me > 0, me - 1, 0),
        ("brick", me < bricks - 1, me + 1, 1),
    )
    floors = (
        ("stack", level > 0, level - 1, 0),
        ("stack", level < stacks - 1, level + 1, 1),
    )

    barrier = pltpu.get_barrier_semaphore()

    def greet(step, carry):
        pl.semaphore_signal(
            barrier, inc=1, device_id={"brick": peer(step)}, device_id_type=pl.DeviceIdType.MESH
        )
        return carry

    lax.fori_loop(1, bricks, greet, 0)
    for axis, there, index, _ in floors:
        @pl.when(there)
        def _():
            pl.semaphore_signal(
                barrier, inc=1, device_id={axis: index}, device_id_type=pl.DeviceIdType.MESH
            )
    pl.semaphore_wait(
        barrier,
        bricks - 1 + jnp.minimum(level, 1) + jnp.minimum(stacks - 1 - level, 1),
    )

    def halo_copy(index, up):
        source = est_hbm.at[:, pl.ds(ROWS - PAD if up else 0, PAD), :]
        return to("brick", index, source, halo.at[1 - up], hsend.at[up], hrecv.at[1 - up])

    for _, there, index, up in sides:
        @pl.when(there)
        def _():
            halo_copy(index, up).start()

    def first(step, c):
        to_index = peer(step)
        return to(
            "brick",
            to_index,
            view_ref.at[pl.ds(c * CHUNK, CHUNK), rows(to_index), :],
            mids[c].at[me],
            send1.at[c, to_index],
            recv1.at[c, me],
        )

    def first_in(step, c):
        source = peer(step)
        return to(
            "brick", source, mids[c].at[source], mids[c].at[source],
            send1.at[c, source], recv1.at[c, source],
        )

    def own(c):
        return pltpu.make_async_copy(
            view_ref.at[pl.ds(c * CHUNK, CHUNK), rows(me), :], mids[c].at[me], local1.at[c]
        )

    def second(step, c):
        to_index = peer(step)
        return to(
            "brick",
            to_index,
            stage.at[to_index, pl.ds(c * CHUNK, CHUNK)],
            owned.at[pl.ds(c * CHUNK, CHUNK), rows(me), :],
            send2.at[c, to_index],
            recv2.at[c, me],
        )

    def second_in(step, c):
        source = peer(step)
        target = owned.at[pl.ds(c * CHUNK, CHUNK), rows(source), :]
        return to("brick", source, target, target, send2.at[c, source], recv2.at[c, source])

    def each(make, act, c):
        def body(step, carry):
            act(make(step, c))
            return carry

        lax.fori_loop(1, bricks, body, 0)

    for c in range(CHUNKS):
        own(c).start()
        each(first, lambda copy: copy.start(), c)

    build_forward(taps_ref, wz, wy, wx)

    for z in (0, EDEPTH - 1):
        ext[z * EROWS : (z + 1) * EROWS, :] = jnp.zeros((EROWS, WIDTH), F32)
    for _, there, _, up in floors:
        @pl.when(jnp.logical_not(there))
        def _():
            start = (PAD + DEPTH) * EROWS if up else EROWS
            ext[start : start + EDGE, :] = jnp.zeros((EDGE, WIDTH), F32)
    for _, there, index, up in sides:
        @pl.when(there)
        def _():
            to(
                "brick", index, halo.at[up], halo.at[up], hsend.at[up], hrecv.at[up]
            ).wait_recv()

        @pl.when(jnp.logical_not(there))
        def _():
            halo[up] = jnp.zeros((DEPTH, PAD, WIDTH), F32)
    for z in range(DEPTH):
        base = (PAD + z) * EROWS
        ext[base : base + PAD, :] = halo[0, z]
        ext[base + PAD : base + PAD + ROWS, :] = est_ref[z]
        ext[base + PAD + ROWS : base + EROWS, :] = halo[1, z]

    def slab_copy(index, up):
        start = (PAD + 1 if up else PAD) * EROWS
        target = EROWS if up else (PAD + DEPTH) * EROWS
        return to(
            "stack", index, ext.at[pl.ds(start, EDGE), :], ext.at[pl.ds(target, EDGE), :],
            ssend.at[up], srecv.at[1 - up],
        )

    for _, there, index, up in floors:
        @pl.when(there)
        def _():
            slab_copy(index, up).start()
    build_backward(taps_ref, bz, by, bx, wide)
    for _, there, index, up in floors:
        @pl.when(there)
        def _():
            start = (PAD + DEPTH) * EROWS if up else EROWS
            target = ext.at[pl.ds(start, EDGE), :]
            to("stack", index, target, target, ssend.at[up], srecv.at[up]).wait_recv()
    axial_forward(ext, wz, axial)

    for c in range(CHUNKS):
        own(c).wait()
        each(first_in, lambda copy: copy.wait_recv(), c)

        def pick(target, carry, c=c):
            for k in range(CHUNK):
                view = c * CHUNK + k
                source = lax.rem(target + bricks - offsets_ref[view], bricks)
                stage[target, view] = mids[c][source, k]
            return carry

        lax.fori_loop(0, bricks, pick, 0)
        each(second, lambda copy: copy.start(), c)
        for k in range(CHUNK):
            view = c * CHUNK + k
            owned[view, rows(me), :] = stage[me, view]

        def one(view, carry):
            lateral_forward(view, axial, wy, side)
            blur[view] = dot(stacked(side[...], 1), wx[view])
            return carry

        lax.fori_loop(c * CHUNK, (c + 1) * CHUNK, one, 0)

    for c in range(CHUNKS):
        each(second_in, lambda copy: copy.wait_recv(), c)

        def one(view, carry):
            cover = cover_ref[view, 0].astype(F32)
            ratio = cover * owned[view] / blur[view]
            side[...] = dot(stacked(ratio, 1), bx[view])
            lateral_backward(view, side, by, back)
            return carry

        lax.fori_loop(c * CHUNK, (c + 1) * CHUNK, one, 0)
    axial_backward(back, bz, spill)

    def spill_copy(index, up):
        start = (PAD + DEPTH) * EROWS if up else EROWS
        return to(
            "stack", index, spill.at[pl.ds(start, EDGE), :], from_stack.at[1 - up],
            tsend.at[up], trecv.at[1 - up],
        )

    for _, there, index, up in floors:
        @pl.when(there)
        def _():
            spill_copy(index, up).start()
    for _, there, index, up in floors:
        @pl.when(there)
        def _():
            to(
                "stack", index, from_stack.at[up], from_stack.at[up], tsend.at[up], trecv.at[up]
            ).wait_recv()
            start = (PAD + 1 if up else PAD) * EROWS
            spill[start : start + EDGE, :] += from_stack[up]
            spill_copy(index, up).wait_send()
    for z in range(DEPTH):
        base = (PAD + z) * EROWS
        to_brick[0, z] = spill[base : base + PAD, :]
        to_brick[1, z] = spill[base + PAD + ROWS : base + EROWS, :]

    def side_copy(index, up):
        return to(
            "brick", index, to_brick.at[up], from_brick.at[1 - up], usend.at[up], urecv.at[1 - up]
        )

    for _, there, index, up in sides:
        @pl.when(there)
        def _():
            side_copy(index, up).start()
    count = jnp.float32(0.0)
    for view in range(VIEWS):
        count = count + cover_ref[view, 0].astype(F32)

    for c in range(CHUNKS):
        each(first, lambda copy: copy.wait_send(), c)
        each(second, lambda copy: copy.wait_send(), c)
    for _, there, index, up in sides:
        @pl.when(there)
        def _():
            halo_copy(index, up).wait_send()
    for _, there, index, up in floors:
        @pl.when(there)
        def _():
            slab_copy(index, up).wait_send()
    for _, there, index, up in sides:
        @pl.when(there)
        def _():
            to(
                "brick", index, from_brick.at[up], from_brick.at[up], usend.at[up], urecv.at[up]
            ).wait_recv()
            side_copy(index, up).wait_send()

        @pl.when(jnp.logical_not(there))
        def _():
            from_brick[up] = jnp.zeros((DEPTH, PAD, WIDTH), F32)
    for z in range(DEPTH):
        base = (PAD + z) * EROWS + PAD
        half = ROWS - PAD
        low = spill[base : base + half, :] + from_brick[0, z]
        high = spill[base + half : base + ROWS, :] + from_brick[1, z]
        out_ref[z, 0:half, :] = est_ref[z, 0:half, :] * low / count
        out_ref[z, half:ROWS, :] = est_ref[z, half:ROWS, :] * high / count


def shards(estimate, view_data, psf_taps, offsets, coverage):
    bricks = lax.axis_size("brick")
    stacks = lax.axis_size("stack")
    part = CELLS // bricks
    vmem = lambda *shape: pltpu.VMEM(shape, F32)
    half = lambda *shape: pltpu.VMEM(shape, BF16)
    sems = lambda *shape: pltpu.SemaphoreType.DMA(shape)
    scratch = [vmem(bricks, CHUNK, part, WIDTH)] * CHUNKS
    scratch += [
        vmem(bricks, VIEWS, part, WIDTH),
        vmem(VIEWS, CELLS, WIDTH),
        vmem(2, DEPTH, PAD, WIDTH),
        vmem(EDEPTH * EROWS, WIDTH),
        half(VIEWS * DEPTH, 3 * EDEPTH),
        half(VIEWS, ROWS, 3 * EROWS),
        half(VIEWS, 3 * WIDTH, WIDTH),
        vmem(VIEWS * SLAB, WIDTH),
        vmem(CELLS, WIDTH),
        vmem(VIEWS, CELLS, WIDTH),
        half(EDEPTH, 3 * VIEWS * DEPTH),
        half(VIEWS, EROWS, 3 * ROWS),
        half(VIEWS, 3 * WIDTH, WIDTH),
        vmem(EDEPTH, 3 * VIEWS * DEPTH),
        vmem(VIEWS * SLAB, WIDTH),
        vmem(EDEPTH * EROWS, WIDTH),
        vmem(2, EDGE, WIDTH),
        vmem(2, DEPTH, PAD, WIDTH),
        vmem(2, DEPTH, PAD, WIDTH),
        sems(CHUNKS, bricks),
        sems(CHUNKS, bricks),
        sems(CHUNKS),
        sems(CHUNKS, bricks),
        sems(CHUNKS, bricks),
    ]
    scratch += [sems(2)] * 8
    return pl.pallas_call(
        functools.partial(kernel, bricks, stacks),
        out_shape=jax.ShapeDtypeStruct(estimate.shape, F32),
        in_specs=[SMEM, SMEM, SMEM, ANY, VMEM, ANY],
        out_specs=VMEM,
        scratch_shapes=scratch,
        compiler_params=pltpu.CompilerParams(
            collective_id=0, has_side_effects=True, vmem_limit_bytes=48 * 1024 * 1024
        ),
    )(
        psf_taps, offsets, coverage, estimate, estimate,
        view_data.reshape(VIEWS, CELLS, WIDTH),
    )


def solution(mesh):
    placed = (
        P("stack", "brick", None),
        P(None, "stack", "brick", None),
        P(),
        P(),
        P(None, "brick"),
    )
    return jax.shard_map(
        shards, mesh=mesh, in_specs=placed, out_specs=P("stack", "brick", None), check_vma=False
    )
```

```python
import functools

import jax
import jax.numpy as jnp
from jax import lax
from jax.experimental import pallas as pl
from jax.experimental.pallas import tpu as pltpu
from jax.sharding import PartitionSpec as P

VIEWS = 6
TAPS = 31
HALF = 15
WIDTH = 128
ROWS = 32
DEPTH = 16
PAD = 16
EROWS = ROWS + 2 * PAD
EDEPTH = DEPTH + 2 * PAD
F32 = jnp.float32
BF16 = jnp.bfloat16


def split(x):
    hi = x.astype(BF16)
    lo = (x - hi.astype(F32)).astype(BF16)
    return hi, lo


def iota(shape, dim):
    return lax.broadcasted_iota(jnp.int32, shape, dim)


def spread_taps(distance, taps_ref, view, dim):
    total = jnp.float32(0.0)
    matrix = jnp.zeros(distance.shape, F32)
    for tap in range(TAPS):
        value = taps_ref[view, dim, tap]
        total = total + value
        matrix = jnp.where(distance == tap, value, matrix)
    return matrix / total


def hi_hi_lo(matrix, part):
    hi, lo = split(matrix)
    return jnp.where(part < 2, hi.astype(F32), lo.astype(F32)).astype(BF16)


def build_forward(taps_ref, wz_ref, wy_ref, wx_ref):
    def one(view, carry):
        col = iota((DEPTH, 3 * EDEPTH), 1)
        dist = col % EDEPTH - iota((DEPTH, 3 * EDEPTH), 0) - 1
        wz_ref[pl.ds(pl.multiple_of(view * DEPTH, DEPTH), DEPTH), :] = hi_hi_lo(
            spread_taps(dist, taps_ref, view, 0), col // EDEPTH
        )
        col = iota((ROWS, 3 * EROWS), 1)
        dist = col % EROWS - iota((ROWS, 3 * EROWS), 0) - 1
        wy_ref[view] = hi_hi_lo(spread_taps(dist, taps_ref, view, 1), col // EROWS)
        dist = iota((WIDTH, WIDTH), 0) - iota((WIDTH, WIDTH), 1) + HALF
        hi, lo = split(spread_taps(dist, taps_ref, view, 2))
        wx_ref[view, 0:WIDTH] = hi
        wx_ref[view, WIDTH : 2 * WIDTH] = hi
        wx_ref[view, 2 * WIDTH : 3 * WIDTH] = lo
        return carry

    lax.fori_loop(0, VIEWS, one, 0)


def build_backward(taps_ref, wz_ref, wy_ref, wx_ref, wide_ref):
    wide_ref[...] = jnp.zeros_like(wide_ref)

    def one(view, carry):
        shape = wide_ref.shape[1:]
        inner = iota(shape, 1) % (CHUNK * DEPTH) - view % CHUNK * DEPTH
        dist = iota(shape, 0) - inner - 1
        dist = jnp.where((inner >= 0) & (inner < DEPTH), dist, -1)
        wide_ref[view // CHUNK] += spread_taps(dist, taps_ref, view, 0)
        col = iota((EROWS, 3 * ROWS), 1)
        dist = iota((EROWS, 3 * ROWS), 0) - col % ROWS - 1
        wy_ref[view] = hi_hi_lo(spread_taps(dist, taps_ref, view, 1), col // ROWS)
        dist = iota((WIDTH, WIDTH), 1) - iota((WIDTH, WIDTH), 0) + HALF
        hi, lo = split(spread_taps(dist, taps_ref, view, 2))
        wx_ref[view, 0:WIDTH] = hi
        wx_ref[view, WIDTH : 2 * WIDTH] = hi
        wx_ref[view, 2 * WIDTH : 3 * WIDTH] = lo
        return carry

    lax.fori_loop(0, VIEWS, one, 0)
    wz_ref[...] = hi_hi_lo(wide_ref[...], iota(wide_ref.shape, 2) // (CHUNK * DEPTH))


def stacked(x, axis):
    hi, lo = split(x)
    return jnp.concatenate([hi, lo, hi], axis=axis)


def dot(a, b):
    return jnp.dot(a, b, preferred_element_type=F32)


def axial_forward(ext_ref, wz_ref, axial_ref):
    def one(step, carry):
        for inner in range(2):
            y = step * 4 + inner * 2
            field = jnp.concatenate(
                [ext_ref[pl.ds(y + k, EDEPTH, stride=EROWS), :] for k in range(2)], axis=1
            )
            out = dot(wz_ref[...], stacked(field, 0))
            for k in range(2):
                axial_ref[pl.ds(y + k, VIEWS * DEPTH, stride=EROWS), :] = out[
                    :, k * WIDTH : (k + 1) * WIDTH
                ]
        return carry

    lax.fori_loop(0, EROWS // 4, one, 0)


def lateral_forward(view, axial_ref, wy_ref, side_ref):
    for z in range(0, DEPTH, 2):
        base = (view * DEPTH + z) * EROWS
        field = jnp.concatenate(
            [
                axial_ref[pl.ds(pl.multiple_of(base + k * EROWS, EROWS), EROWS), :]
                for k in range(2)
            ],
            axis=1,
        )
        out = dot(wy_ref[view], stacked(field, 0))
        for k in range(2):
            side_ref[(z + k) * ROWS : (z + k + 1) * ROWS, :] = out[
                :, k * WIDTH : (k + 1) * WIDTH
            ]


def lateral_backward(view, side_ref, wy_ref, back_ref):
    for z in range(0, DEPTH, 2):
        field = jnp.concatenate(
            [side_ref[(z + k) * ROWS : (z + k + 1) * ROWS, :] for k in range(2)], axis=1
        )
        out = dot(wy_ref[view], stacked(field, 0))
        base = (view * DEPTH + z) * EROWS
        for k in range(2):
            back_ref[pl.ds(pl.multiple_of(base + k * EROWS, EROWS), EROWS), :] = out[
                :, k * WIDTH : (k + 1) * WIDTH
            ]


def axial_backward(c, edges, back_ref, wz_ref, out_ref):
    half = ROWS // 2

    def one(step, carry):
        for inner in range(2):
            spot = step * 4 + inner * 2
            y = spot + (jnp.where(step >= half // 4, ROWS, 0) if edges else PAD)
            field = jnp.concatenate(
                [
                    back_ref[pl.ds(c * CHUNK * SLAB + y + k, CHUNK * DEPTH, stride=EROWS), :]
                    for k in range(2)
                ],
                axis=1,
            )
            out = dot(wz_ref[c], stacked(field, 0))
            for k in range(2):
                place = pl.ds(spot + k, EDEPTH, stride=ROWS)
                part = out[:, k * WIDTH : (k + 1) * WIDTH]
                out_ref[place, :] = part if c == 0 else out_ref[place, :] + part
        return carry

    lax.fori_loop(0, ROWS // 4, one, 0)


CHUNK = 2
CHUNKS = VIEWS // CHUNK
CELLS = DEPTH * ROWS
SLAB = DEPTH * EROWS
EDGE = HALF * EROWS
BAND = HALF * ROWS
ANY = pl.BlockSpec(memory_space=pl.ANY)
VMEM = pl.BlockSpec(memory_space=pltpu.VMEM)
SMEM = pl.BlockSpec(memory_space=pltpu.SMEM)


def kernel(
    bricks, stacks, taps_ref, flags_ref, est_hbm, view_ref, out_ref, est_ref,
    mid0, mid1, mid2, stage, owned,
    halo, ext, wz, wy, wx, axial, side, blur,
    bz, by, bx, wide, back, spill_edges, spill_middle, from_edges, from_middle, to_brick, from_brick,
    send1, recv1, local1, send2, recv2, hsend, hrecv, ssend, srecv, tsend, trecv, usend, urecv, msend, mrecv, esem,
):
    mids = (mid0, mid1, mid2)
    me = lax.axis_index("brick")
    level = lax.axis_index("stack")
    part = CELLS // bricks

    def to(axis, index, source, target, send_sem, recv_sem):
        return pltpu.make_async_remote_copy(
            src_ref=source,
            dst_ref=target,
            send_sem=send_sem,
            recv_sem=recv_sem,
            device_id={axis: index},
            device_id_type=pl.DeviceIdType.MESH,
        )

    def peer(step):
        turn = lax.rem(step - 1 + lax.rem(level, 2) * (bricks // 2 - 1), bricks - 1)
        return lax.rem(me + 1 + turn, bricks)

    def rows(index):
        return pl.ds(pl.multiple_of(index * part, part), part)

    sides = (
        ("brick", me > 0, me - 1, 0),
        ("brick", me < bricks - 1, me + 1, 1),
    )
    floors = (
        ("stack", level > 0, level - 1, 0),
        ("stack", level < stacks - 1, level + 1, 1),
    )

    load = pltpu.make_async_copy(est_hbm, est_ref, esem.at[0])
    load.start()
    barrier = pltpu.get_barrier_semaphore()

    def greet(step, carry):
        pl.semaphore_signal(
            barrier, inc=1, device_id={"brick": peer(step)}, device_id_type=pl.DeviceIdType.MESH
        )
        return carry

    lax.fori_loop(1, bricks, greet, 0)
    for axis, there, index, _ in floors:
        @pl.when(there)
        def _():
            pl.semaphore_signal(
                barrier, inc=1, device_id={axis: index}, device_id_type=pl.DeviceIdType.MESH
            )
    pl.semaphore_wait(
        barrier,
        bricks - 1 + jnp.minimum(level, 1) + jnp.minimum(stacks - 1 - level, 1),
    )

    def halo_copy(index, up):
        source = est_hbm.at[:, pl.ds(ROWS - PAD if up else 0, PAD), :]
        return to("brick", index, source, halo.at[1 - up], hsend.at[up], hrecv.at[1 - up])

    for _, there, index, up in sides:
        @pl.when(there)
        def _():
            halo_copy(index, up).start()

    def first(step, c):
        to_index = peer(step)
        return to(
            "brick",
            to_index,
            view_ref.at[pl.ds(c * CHUNK, CHUNK), rows(to_index), :],
            mids[c].at[me],
            send1.at[c, to_index],
            recv1.at[c, me],
        )

    def first_in(step, c):
        source = peer(step)
        return to(
            "brick", source, mids[c].at[source], mids[c].at[source],
            send1.at[c, source], recv1.at[c, source],
        )

    def own(c):
        return pltpu.make_async_copy(
            view_ref.at[pl.ds(c * CHUNK, CHUNK), rows(me), :], mids[c].at[me], local1.at[c]
        )

    def second(step, c):
        to_index = peer(step)
        return to(
            "brick",
            to_index,
            stage.at[to_index, pl.ds(c * CHUNK, CHUNK)],
            owned.at[pl.ds(c * CHUNK, CHUNK), rows(me), :],
            send2.at[c, to_index],
            recv2.at[c, me],
        )

    def second_in(step, c):
        source = peer(step)
        target = owned.at[pl.ds(c * CHUNK, CHUNK), rows(source), :]
        return to("brick", source, target, target, send2.at[c, source], recv2.at[c, source])

    def each(make, act, c):
        def body(step, carry):
            act(make(step, c))
            return carry

        lax.fori_loop(1, bricks, body, 0)

    for c in range(CHUNKS):
        own(c).start()
        each(first, lambda copy: copy.start(), c)

    build_forward(taps_ref, wz, wy, wx)

    for z in (0, EDEPTH - 1):
        ext[z * EROWS : (z + 1) * EROWS, :] = jnp.zeros((EROWS, WIDTH), F32)
    for _, there, _, up in floors:
        @pl.when(jnp.logical_not(there))
        def _():
            start = (PAD + DEPTH) * EROWS if up else EROWS
            ext[start : start + EDGE, :] = jnp.zeros((EDGE, WIDTH), F32)
    for _, there, index, up in sides:
        @pl.when(there)
        def _():
            to(
                "brick", index, halo.at[up], halo.at[up], hsend.at[up], hrecv.at[up]
            ).wait_recv()

        @pl.when(jnp.logical_not(there))
        def _():
            halo[up] = jnp.zeros((DEPTH, PAD, WIDTH), F32)
    load.wait()
    for z in range(DEPTH):
        base = (PAD + z) * EROWS
        ext[base : base + PAD, :] = halo[0, z]
        ext[base + PAD : base + PAD + ROWS, :] = est_ref[z]
        ext[base + PAD + ROWS : base + EROWS, :] = halo[1, z]

    def slab_copy(index, up):
        start = (PAD + 1 if up else PAD) * EROWS
        target = EROWS if up else (PAD + DEPTH) * EROWS
        return to(
            "stack", index, ext.at[pl.ds(start, EDGE), :], ext.at[pl.ds(target, EDGE), :],
            ssend.at[up], srecv.at[1 - up],
        )

    for _, there, index, up in floors:
        @pl.when(there)
        def _():
            slab_copy(index, up).start()
    build_backward(taps_ref, bz, by, bx, wide)
    for _, there, index, up in floors:
        @pl.when(there)
        def _():
            start = (PAD + DEPTH) * EROWS if up else EROWS
            target = ext.at[pl.ds(start, EDGE), :]
            to("stack", index, target, target, ssend.at[up], srecv.at[up]).wait_recv()
    axial_forward(ext, wz, axial)

    for c in range(CHUNKS):
        own(c).wait()
        each(first_in, lambda copy: copy.wait_recv(), c)

        def pick(target, carry, c=c):
            for k in range(CHUNK):
                view = c * CHUNK + k
                source = lax.rem(target + bricks - flags_ref[view], bricks)
                stage[target, view] = mids[c][source, k]
            return carry

        lax.fori_loop(0, bricks, pick, 0)
        each(second, lambda copy: copy.start(), c)
        for k in range(CHUNK):
            view = c * CHUNK + k
            owned[view, rows(me), :] = stage[me, view]

        def one(view, carry):
            lateral_forward(view, axial, wy, side)
            blur[view] = dot(stacked(side[...], 1), wx[view])
            return carry

        lax.fori_loop(c * CHUNK, (c + 1) * CHUNK, one, 0)

    for c in range(CHUNKS):
        each(second_in, lambda copy: copy.wait_recv(), c)

        def one(view, carry):
            cover = flags_ref[VIEWS + view].astype(F32)
            ratio = cover * owned[view] / blur[view]
            side[...] = dot(stacked(ratio, 1), bx[view])
            lateral_backward(view, side, by, back)
            return carry

        lax.fori_loop(c * CHUNK, (c + 1) * CHUNK, one, 0)
        if c < CHUNKS - 1:
            axial_backward(c, True, back, bz, spill_edges)
            axial_backward(c, False, back, bz, spill_middle)

    def spill_copy(index, up, source, target, send_sem, recv_sem):
        start = (PAD + DEPTH) * ROWS if up else ROWS
        return to(
            "stack", index, source.at[pl.ds(start, BAND), :], target.at[1 - up],
            send_sem.at[up], recv_sem.at[1 - up],
        )

    spills = (
        (True, spill_edges, from_edges, tsend, trecv),
        (False, spill_middle, from_middle, msend, mrecv),
    )
    for edges, source, target, send_sem, recv_sem in spills:
        axial_backward(CHUNKS - 1, edges, back, bz, source)
        for _, there, index, up in floors:
            @pl.when(there)
            def _():
                spill_copy(index, up, source, target, send_sem, recv_sem).start()

    def take(source, target, send_sem, recv_sem):
        for _, there, index, up in floors:
            @pl.when(there)
            def _():
                to(
                    "stack", index, target.at[up], target.at[up], send_sem.at[up], recv_sem.at[up]
                ).wait_recv()
                start = (PAD + 1 if up else PAD) * ROWS
                source[start : start + BAND, :] += target[up]

    take(*spills[0][1:])
    for z in range(DEPTH):
        base = (PAD + z) * ROWS
        to_brick[0, z] = spill_edges[base : base + PAD, :]
        to_brick[1, z] = spill_edges[base + ROWS - PAD : base + ROWS, :]

    def side_copy(index, up):
        return to(
            "brick", index, to_brick.at[up], from_brick.at[1 - up], usend.at[up], urecv.at[1 - up]
        )

    for _, there, index, up in sides:
        @pl.when(there)
        def _():
            side_copy(index, up).start()
    count = jnp.float32(0.0)
    for view in range(VIEWS):
        count = count + flags_ref[VIEWS + view].astype(F32)

    for c in range(CHUNKS):
        each(first, lambda copy: copy.wait_send(), c)
        each(second, lambda copy: copy.wait_send(), c)
    for _, there, index, up in sides:
        @pl.when(there)
        def _():
            halo_copy(index, up).wait_send()
    for _, there, index, up in floors:
        @pl.when(there)
        def _():
            slab_copy(index, up).wait_send()
    take(*spills[1][1:])
    for _, there, index, up in floors:
        @pl.when(there)
        def _():
            for _, source, target, send_sem, recv_sem in spills:
                spill_copy(index, up, source, target, send_sem, recv_sem).wait_send()
    for _, there, index, up in sides:
        @pl.when(there)
        def _():
            to(
                "brick", index, from_brick.at[up], from_brick.at[up], usend.at[up], urecv.at[up]
            ).wait_recv()
            side_copy(index, up).wait_send()

        @pl.when(jnp.logical_not(there))
        def _():
            from_brick[up] = jnp.zeros((DEPTH, PAD, WIDTH), F32)
    for z in range(DEPTH):
        base = (PAD + z) * ROWS
        half = ROWS - PAD
        low = spill_middle[base : base + half, :] + from_brick[0, z]
        high = spill_middle[base + half : base + ROWS, :] + from_brick[1, z]
        out_ref[z, 0:half, :] = est_ref[z, 0:half, :] * low / count
        out_ref[z, half:ROWS, :] = est_ref[z, half:ROWS, :] * high / count


def shards(estimate, view_data, psf_taps, offsets, coverage):
    bricks = lax.axis_size("brick")
    stacks = lax.axis_size("stack")
    part = CELLS // bricks
    vmem = lambda *shape: pltpu.VMEM(shape, F32)
    half = lambda *shape: pltpu.VMEM(shape, BF16)
    sems = lambda *shape: pltpu.SemaphoreType.DMA(shape)
    scratch = [vmem(*estimate.shape)] + [vmem(bricks, CHUNK, part, WIDTH)] * CHUNKS
    scratch += [
        vmem(bricks, VIEWS, part, WIDTH),
        vmem(VIEWS, CELLS, WIDTH),
        vmem(2, DEPTH, PAD, WIDTH),
        vmem(EDEPTH * EROWS, WIDTH),
        half(VIEWS * DEPTH, 3 * EDEPTH),
        half(VIEWS, ROWS, 3 * EROWS),
        half(VIEWS, 3 * WIDTH, WIDTH),
        vmem(VIEWS * SLAB, WIDTH),
        vmem(CELLS, WIDTH),
        vmem(VIEWS, CELLS, WIDTH),
        half(CHUNKS, EDEPTH, 3 * CHUNK * DEPTH),
        half(VIEWS, EROWS, 3 * ROWS),
        half(VIEWS, 3 * WIDTH, WIDTH),
        vmem(CHUNKS, EDEPTH, 3 * CHUNK * DEPTH),
        vmem(VIEWS * SLAB, WIDTH),
        vmem(EDEPTH * ROWS, WIDTH),
        vmem(EDEPTH * ROWS, WIDTH),
        vmem(2, BAND, WIDTH),
        vmem(2, BAND, WIDTH),
        vmem(2, DEPTH, PAD, WIDTH),
        vmem(2, DEPTH, PAD, WIDTH),
        sems(CHUNKS, bricks),
        sems(CHUNKS, bricks),
        sems(CHUNKS),
        sems(CHUNKS, bricks),
        sems(CHUNKS, bricks),
    ]
    scratch += [sems(2)] * 10 + [sems(1)]
    return pl.pallas_call(
        functools.partial(kernel, bricks, stacks),
        out_shape=jax.ShapeDtypeStruct(estimate.shape, F32),
        in_specs=[SMEM, SMEM, ANY, ANY],
        out_specs=VMEM,
        scratch_shapes=scratch,
        compiler_params=pltpu.CompilerParams(
            collective_id=0, has_side_effects=True, vmem_limit_bytes=48 * 1024 * 1024
        ),
    )(
        psf_taps, jnp.concatenate([offsets, coverage[:, 0]]), estimate,
        view_data.reshape(VIEWS, CELLS, WIDTH),
    )


def solution(mesh):
    placed = (
        P("stack", "brick", None),
        P(None, "stack", "brick", None),
        P(),
        P(),
        P(None, "brick"),
    )
    return jax.shard_map(
        shards, mesh=mesh, in_specs=placed, out_specs=P("stack", "brick", None), check_vma=False
    )
```

```python
import functools

import jax
import jax.numpy as jnp
from jax import lax
from jax.experimental import pallas as pl
from jax.experimental.pallas import tpu as pltpu
from jax.sharding import PartitionSpec as P

VIEWS = 6
TAPS = 31
HALF = 15
WIDTH = 128
ROWS = 32
DEPTH = 16
PAD = 16
EROWS = ROWS + 2 * PAD
EDEPTH = DEPTH + 2 * PAD
F32 = jnp.float32
BF16 = jnp.bfloat16


def split(x):
    hi = x.astype(BF16)
    lo = (x - hi.astype(F32)).astype(BF16)
    return hi, lo


def iota(shape, dim):
    return lax.broadcasted_iota(jnp.int32, shape, dim)


def spread_taps(distance, taps_ref, view, dim):
    total = jnp.float32(0.0)
    matrix = jnp.zeros(distance.shape, F32)
    for tap in range(TAPS):
        value = taps_ref[view, dim, tap]
        total = total + value
        matrix = jnp.where(distance == tap, value, matrix)
    return matrix / total


def hi_hi_lo(matrix, part):
    hi, lo = split(matrix)
    return jnp.where(part < 2, hi.astype(F32), lo.astype(F32)).astype(BF16)


def build_forward(taps_ref, wz_ref, wy_ref, wx_ref):
    def one(view, carry):
        col = iota((DEPTH, 3 * EDEPTH), 1)
        dist = col % EDEPTH - iota((DEPTH, 3 * EDEPTH), 0) - 1
        wz_ref[pl.ds(pl.multiple_of(view * DEPTH, DEPTH), DEPTH), :] = hi_hi_lo(
            spread_taps(dist, taps_ref, view, 0), col // EDEPTH
        )
        col = iota((ROWS, 3 * EROWS), 1)
        dist = col % EROWS - iota((ROWS, 3 * EROWS), 0) - 1
        wy_ref[view] = hi_hi_lo(spread_taps(dist, taps_ref, view, 1), col // EROWS)
        dist = iota((WIDTH, WIDTH), 0) - iota((WIDTH, WIDTH), 1) + HALF
        hi, lo = split(spread_taps(dist, taps_ref, view, 2))
        wx_ref[view, 0:WIDTH] = hi
        wx_ref[view, WIDTH : 2 * WIDTH] = hi
        wx_ref[view, 2 * WIDTH : 3 * WIDTH] = lo
        return carry

    lax.fori_loop(0, VIEWS, one, 0)


def build_backward(taps_ref, wz_ref, wy_ref, wx_ref, wide_ref):
    wide_ref[...] = jnp.zeros_like(wide_ref)

    def one(view, carry):
        shape = wide_ref.shape[1:]
        inner = iota(shape, 1) % (CHUNK * DEPTH) - view % CHUNK * DEPTH
        dist = iota(shape, 0) - inner - 1
        dist = jnp.where((inner >= 0) & (inner < DEPTH), dist, -1)
        wide_ref[view // CHUNK] += spread_taps(dist, taps_ref, view, 0)
        col = iota((EROWS, 3 * ROWS), 1)
        dist = iota((EROWS, 3 * ROWS), 0) - col % ROWS - 1
        wy_ref[view] = hi_hi_lo(spread_taps(dist, taps_ref, view, 1), col // ROWS)
        dist = iota((WIDTH, WIDTH), 1) - iota((WIDTH, WIDTH), 0) + HALF
        hi, lo = split(spread_taps(dist, taps_ref, view, 2))
        wx_ref[view, 0:WIDTH] = hi
        wx_ref[view, WIDTH : 2 * WIDTH] = hi
        wx_ref[view, 2 * WIDTH : 3 * WIDTH] = lo
        return carry

    lax.fori_loop(0, VIEWS, one, 0)
    wz_ref[...] = hi_hi_lo(wide_ref[...], iota(wide_ref.shape, 2) // (CHUNK * DEPTH))


def stacked(x, axis):
    hi, lo = split(x)
    return jnp.concatenate([hi, lo, hi], axis=axis)


def dot(a, b):
    return jnp.dot(a, b, preferred_element_type=F32)


def axial_forward(ext_ref, wz_ref, axial_ref):
    def one(step, carry):
        for inner in range(2):
            y = step * 4 + inner * 2
            field = jnp.concatenate(
                [ext_ref[pl.ds(y + k, EDEPTH, stride=EROWS), :] for k in range(2)], axis=1
            )
            out = dot(wz_ref[...], stacked(field, 0))
            for k in range(2):
                axial_ref[pl.ds(y + k, VIEWS * DEPTH, stride=EROWS), :] = out[
                    :, k * WIDTH : (k + 1) * WIDTH
                ]
        return carry

    lax.fori_loop(0, EROWS // 4, one, 0)


def lateral_forward(view, axial_ref, wy_ref, side_ref):
    for z in range(0, DEPTH, 2):
        base = (view * DEPTH + z) * EROWS
        field = jnp.concatenate(
            [
                axial_ref[pl.ds(pl.multiple_of(base + k * EROWS, EROWS), EROWS), :]
                for k in range(2)
            ],
            axis=1,
        )
        out = dot(wy_ref[view], stacked(field, 0))
        for k in range(2):
            side_ref[(z + k) * ROWS : (z + k + 1) * ROWS, :] = out[
                :, k * WIDTH : (k + 1) * WIDTH
            ]


def lateral_backward(view, side_ref, wy_ref, back_ref):
    for z in range(0, DEPTH, 2):
        field = jnp.concatenate(
            [side_ref[(z + k) * ROWS : (z + k + 1) * ROWS, :] for k in range(2)], axis=1
        )
        out = dot(wy_ref[view], stacked(field, 0))
        base = (view * DEPTH + z) * EROWS
        for k in range(2):
            back_ref[pl.ds(pl.multiple_of(base + k * EROWS, EROWS), EROWS), :] = out[
                :, k * WIDTH : (k + 1) * WIDTH
            ]


def axial_backward(c, edges, back_ref, wz_ref, out_ref):
    half = ROWS // 2

    def one(step, carry):
        for inner in range(2):
            spot = step * 4 + inner * 2
            y = spot + (jnp.where(step >= half // 4, ROWS, 0) if edges else PAD)
            field = jnp.concatenate(
                [
                    back_ref[pl.ds(c * CHUNK * SLAB + y + k, CHUNK * DEPTH, stride=EROWS), :]
                    for k in range(2)
                ],
                axis=1,
            )
            out = dot(wz_ref[c], stacked(field, 0))
            for k in range(2):
                place = pl.ds(spot + k, EDEPTH, stride=ROWS)
                part = out[:, k * WIDTH : (k + 1) * WIDTH]
                out_ref[place, :] = part if c == 0 else out_ref[place, :] + part
        return carry

    lax.fori_loop(0, ROWS // 4, one, 0)


CHUNK = 1
CHUNKS = VIEWS // CHUNK
CELLS = DEPTH * ROWS
SLAB = DEPTH * EROWS
EDGE = HALF * EROWS
BAND = HALF * ROWS
ANY = pl.BlockSpec(memory_space=pl.ANY)
VMEM = pl.BlockSpec(memory_space=pltpu.VMEM)
SMEM = pl.BlockSpec(memory_space=pltpu.SMEM)


def kernel(
    bricks, stacks, taps_ref, flags_ref, est_hbm, view_ref, out_ref, est_ref,
    mid0, mid1, mid2, mid3, mid4, mid5, stage, owned,
    halo, ext, wz, wy, wx, axial, side, blur,
    bz, by, bx, wide, back, spill_edges, spill_middle, from_edges, from_middle, to_brick, from_brick,
    send1, recv1, local1, send2, recv2, hsend, hrecv, ssend, srecv, tsend, trecv, usend, urecv, msend, mrecv, esem,
):
    mids = (mid0, mid1, mid2, mid3, mid4, mid5)
    me = lax.axis_index("brick")
    level = lax.axis_index("stack")
    part = CELLS // bricks

    def to(axis, index, source, target, send_sem, recv_sem):
        return pltpu.make_async_remote_copy(
            src_ref=source,
            dst_ref=target,
            send_sem=send_sem,
            recv_sem=recv_sem,
            device_id={axis: index},
            device_id_type=pl.DeviceIdType.MESH,
        )

    def peer(step):
        turn = lax.rem(step - 1 + lax.rem(level, 2) * (bricks // 2 - 1), bricks - 1)
        return lax.rem(me + 1 + turn, bricks)

    def rows(index):
        return pl.ds(pl.multiple_of(index * part, part), part)

    sides = (
        ("brick", me > 0, me - 1, 0),
        ("brick", me < bricks - 1, me + 1, 1),
    )
    floors = (
        ("stack", level > 0, level - 1, 0),
        ("stack", level < stacks - 1, level + 1, 1),
    )

    load = pltpu.make_async_copy(est_hbm, est_ref, esem.at[0])
    load.start()
    barrier = pltpu.get_barrier_semaphore()

    def greet(step, carry):
        pl.semaphore_signal(
            barrier, inc=1, device_id={"brick": peer(step)}, device_id_type=pl.DeviceIdType.MESH
        )
        return carry

    lax.fori_loop(1, bricks, greet, 0)
    for axis, there, index, _ in floors:
        @pl.when(there)
        def _():
            pl.semaphore_signal(
                barrier, inc=1, device_id={axis: index}, device_id_type=pl.DeviceIdType.MESH
            )
    pl.semaphore_wait(
        barrier,
        bricks - 1 + jnp.minimum(level, 1) + jnp.minimum(stacks - 1 - level, 1),
    )

    def halo_copy(index, up):
        source = est_hbm.at[:, pl.ds(ROWS - PAD if up else 0, PAD), :]
        return to("brick", index, source, halo.at[1 - up], hsend.at[up], hrecv.at[1 - up])

    for _, there, index, up in sides:
        @pl.when(there)
        def _():
            halo_copy(index, up).start()

    def first(step, c):
        to_index = peer(step)
        return to(
            "brick",
            to_index,
            view_ref.at[pl.ds(c * CHUNK, CHUNK), rows(to_index), :],
            mids[c].at[me],
            send1.at[c, to_index],
            recv1.at[c, me],
        )

    def first_in(step, c):
        source = peer(step)
        return to(
            "brick", source, mids[c].at[source], mids[c].at[source],
            send1.at[c, source], recv1.at[c, source],
        )

    def own(c):
        return pltpu.make_async_copy(
            view_ref.at[pl.ds(c * CHUNK, CHUNK), rows(me), :], mids[c].at[me], local1.at[c]
        )

    def second(step, c):
        to_index = peer(step)
        return to(
            "brick",
            to_index,
            stage.at[to_index, pl.ds(c * CHUNK, CHUNK)],
            owned.at[pl.ds(c * CHUNK, CHUNK), rows(me), :],
            send2.at[c, to_index],
            recv2.at[c, me],
        )

    def second_in(step, c):
        source = peer(step)
        target = owned.at[pl.ds(c * CHUNK, CHUNK), rows(source), :]
        return to("brick", source, target, target, send2.at[c, source], recv2.at[c, source])

    def each(make, act, c):
        def body(step, carry):
            act(make(step, c))
            return carry

        lax.fori_loop(1, bricks, body, 0)

    for c in range(CHUNKS):
        own(c).start()
        each(first, lambda copy: copy.start(), c)

    build_forward(taps_ref, wz, wy, wx)

    for z in (0, EDEPTH - 1):
        ext[z * EROWS : (z + 1) * EROWS, :] = jnp.zeros((EROWS, WIDTH), F32)
    for _, there, _, up in floors:
        @pl.when(jnp.logical_not(there))
        def _():
            start = (PAD + DEPTH) * EROWS if up else EROWS
            ext[start : start + EDGE, :] = jnp.zeros((EDGE, WIDTH), F32)
    for _, there, index, up in sides:
        @pl.when(there)
        def _():
            to(
                "brick", index, halo.at[up], halo.at[up], hsend.at[up], hrecv.at[up]
            ).wait_recv()

        @pl.when(jnp.logical_not(there))
        def _():
            halo[up] = jnp.zeros((DEPTH, PAD, WIDTH), F32)
    load.wait()
    for z in range(DEPTH):
        base = (PAD + z) * EROWS
        ext[base : base + PAD, :] = halo[0, z]
        ext[base + PAD : base + PAD + ROWS, :] = est_ref[z]
        ext[base + PAD + ROWS : base + EROWS, :] = halo[1, z]

    def slab_copy(index, up):
        start = (PAD + 1 if up else PAD) * EROWS
        target = EROWS if up else (PAD + DEPTH) * EROWS
        return to(
            "stack", index, ext.at[pl.ds(start, EDGE), :], ext.at[pl.ds(target, EDGE), :],
            ssend.at[up], srecv.at[1 - up],
        )

    for _, there, index, up in floors:
        @pl.when(there)
        def _():
            slab_copy(index, up).start()
    build_backward(taps_ref, bz, by, bx, wide)
    for _, there, index, up in floors:
        @pl.when(there)
        def _():
            start = (PAD + DEPTH) * EROWS if up else EROWS
            target = ext.at[pl.ds(start, EDGE), :]
            to("stack", index, target, target, ssend.at[up], srecv.at[up]).wait_recv()
    axial_forward(ext, wz, axial)

    for c in range(CHUNKS):
        own(c).wait()
        each(first_in, lambda copy: copy.wait_recv(), c)

        def pick(target, carry, c=c):
            for k in range(CHUNK):
                view = c * CHUNK + k
                source = lax.rem(target + bricks - flags_ref[view], bricks)
                stage[target, view] = mids[c][source, k]
            return carry

        lax.fori_loop(0, bricks, pick, 0)
        each(second, lambda copy: copy.start(), c)
        for k in range(CHUNK):
            view = c * CHUNK + k
            owned[view, rows(me), :] = stage[me, view]

        def one(view, carry):
            lateral_forward(view, axial, wy, side)
            blur[view] = dot(stacked(side[...], 1), wx[view])
            return carry

        lax.fori_loop(c * CHUNK, (c + 1) * CHUNK, one, 0)

    for c in range(CHUNKS):
        each(second_in, lambda copy: copy.wait_recv(), c)

        def one(view, carry):
            cover = flags_ref[VIEWS + view].astype(F32)
            ratio = cover * owned[view] / blur[view]
            side[...] = dot(stacked(ratio, 1), bx[view])
            lateral_backward(view, side, by, back)
            return carry

        lax.fori_loop(c * CHUNK, (c + 1) * CHUNK, one, 0)
        if c < CHUNKS - 1:
            axial_backward(c, True, back, bz, spill_edges)
            axial_backward(c, False, back, bz, spill_middle)

    def spill_copy(index, up, source, target, send_sem, recv_sem):
        start = (PAD + DEPTH) * ROWS if up else ROWS
        return to(
            "stack", index, source.at[pl.ds(start, BAND), :], target.at[1 - up],
            send_sem.at[up], recv_sem.at[1 - up],
        )

    spills = (
        (True, spill_edges, from_edges, tsend, trecv),
        (False, spill_middle, from_middle, msend, mrecv),
    )
    for edges, source, target, send_sem, recv_sem in spills:
        axial_backward(CHUNKS - 1, edges, back, bz, source)
        for _, there, index, up in floors:
            @pl.when(there)
            def _():
                spill_copy(index, up, source, target, send_sem, recv_sem).start()

    def take(source, target, send_sem, recv_sem):
        for _, there, index, up in floors:
            @pl.when(there)
            def _():
                to(
                    "stack", index, target.at[up], target.at[up], send_sem.at[up], recv_sem.at[up]
                ).wait_recv()
                start = (PAD + 1 if up else PAD) * ROWS
                source[start : start + BAND, :] += target[up]

    take(*spills[0][1:])
    for z in range(DEPTH):
        base = (PAD + z) * ROWS
        to_brick[0, z] = spill_edges[base : base + PAD, :]
        to_brick[1, z] = spill_edges[base + ROWS - PAD : base + ROWS, :]

    def side_copy(index, up):
        return to(
            "brick", index, to_brick.at[up], from_brick.at[1 - up], usend.at[up], urecv.at[1 - up]
        )

    for _, there, index, up in sides:
        @pl.when(there)
        def _():
            side_copy(index, up).start()
    count = jnp.float32(0.0)
    for view in range(VIEWS):
        count = count + flags_ref[VIEWS + view].astype(F32)

    for c in range(CHUNKS):
        each(first, lambda copy: copy.wait_send(), c)
        each(second, lambda copy: copy.wait_send(), c)
    for _, there, index, up in sides:
        @pl.when(there)
        def _():
            halo_copy(index, up).wait_send()
    for _, there, index, up in floors:
        @pl.when(there)
        def _():
            slab_copy(index, up).wait_send()
    take(*spills[1][1:])
    for _, there, index, up in floors:
        @pl.when(there)
        def _():
            for _, source, target, send_sem, recv_sem in spills:
                spill_copy(index, up, source, target, send_sem, recv_sem).wait_send()
    for _, there, index, up in sides:
        @pl.when(there)
        def _():
            to(
                "brick", index, from_brick.at[up], from_brick.at[up], usend.at[up], urecv.at[up]
            ).wait_recv()
            side_copy(index, up).wait_send()

        @pl.when(jnp.logical_not(there))
        def _():
            from_brick[up] = jnp.zeros((DEPTH, PAD, WIDTH), F32)
    for z in range(DEPTH):
        base = (PAD + z) * ROWS
        half = ROWS - PAD
        low = spill_middle[base : base + half, :] + from_brick[0, z]
        high = spill_middle[base + half : base + ROWS, :] + from_brick[1, z]
        out_ref[z, 0:half, :] = est_ref[z, 0:half, :] * low / count
        out_ref[z, half:ROWS, :] = est_ref[z, half:ROWS, :] * high / count


def shards(estimate, view_data, psf_taps, offsets, coverage):
    bricks = lax.axis_size("brick")
    stacks = lax.axis_size("stack")
    part = CELLS // bricks
    vmem = lambda *shape: pltpu.VMEM(shape, F32)
    half = lambda *shape: pltpu.VMEM(shape, BF16)
    sems = lambda *shape: pltpu.SemaphoreType.DMA(shape)
    scratch = [vmem(*estimate.shape)] + [vmem(bricks, CHUNK, part, WIDTH)] * CHUNKS
    scratch += [
        vmem(bricks, VIEWS, part, WIDTH),
        vmem(VIEWS, CELLS, WIDTH),
        vmem(2, DEPTH, PAD, WIDTH),
        vmem(EDEPTH * EROWS, WIDTH),
        half(VIEWS * DEPTH, 3 * EDEPTH),
        half(VIEWS, ROWS, 3 * EROWS),
        half(VIEWS, 3 * WIDTH, WIDTH),
        vmem(VIEWS * SLAB, WIDTH),
        vmem(CELLS, WIDTH),
        vmem(VIEWS, CELLS, WIDTH),
        half(CHUNKS, EDEPTH, 3 * CHUNK * DEPTH),
        half(VIEWS, EROWS, 3 * ROWS),
        half(VIEWS, 3 * WIDTH, WIDTH),
        vmem(CHUNKS, EDEPTH, 3 * CHUNK * DEPTH),
        vmem(VIEWS * SLAB, WIDTH),
        vmem(EDEPTH * ROWS, WIDTH),
        vmem(EDEPTH * ROWS, WIDTH),
        vmem(2, BAND, WIDTH),
        vmem(2, BAND, WIDTH),
        vmem(2, DEPTH, PAD, WIDTH),
        vmem(2, DEPTH, PAD, WIDTH),
        sems(CHUNKS, bricks),
        sems(CHUNKS, bricks),
        sems(CHUNKS),
        sems(CHUNKS, bricks),
        sems(CHUNKS, bricks),
    ]
    scratch += [sems(2)] * 10 + [sems(1)]
    return pl.pallas_call(
        functools.partial(kernel, bricks, stacks),
        out_shape=jax.ShapeDtypeStruct(estimate.shape, F32),
        in_specs=[SMEM, SMEM, ANY, ANY],
        out_specs=VMEM,
        scratch_shapes=scratch,
        compiler_params=pltpu.CompilerParams(
            collective_id=0, has_side_effects=True, vmem_limit_bytes=63 * 1024 * 1024
        ),
    )(
        psf_taps, jnp.concatenate([offsets, coverage[:, 0]]), estimate,
        view_data.reshape(VIEWS, CELLS, WIDTH),
    )


def solution(mesh):
    placed = (
        P("stack", "brick", None),
        P(None, "stack", "brick", None),
        P(),
        P(),
        P(None, "brick"),
    )
    return jax.shard_map(
        shards, mesh=mesh, in_specs=placed, out_specs=P("stack", "brick", None), check_vma=False
    )
```

```python
import functools

import jax
import jax.numpy as jnp
from jax import lax
from jax.experimental import pallas as pl
from jax.experimental.pallas import tpu as pltpu
from jax.sharding import PartitionSpec as P

VIEWS = 6
TAPS = 31
HALF = 15
WIDTH = 128
ROWS = 32
DEPTH = 16
PAD = 16
EROWS = ROWS + 2 * PAD
EDEPTH = DEPTH + 2 * PAD
F32 = jnp.float32
BF16 = jnp.bfloat16


def split(x):
    hi = x.astype(BF16)
    lo = (x - hi.astype(F32)).astype(BF16)
    return hi, lo


def iota(shape, dim):
    return lax.broadcasted_iota(jnp.int32, shape, dim)


def spread_taps(distance, taps_ref, view, dim):
    total = jnp.float32(0.0)
    matrix = jnp.zeros(distance.shape, F32)
    for tap in range(TAPS):
        value = taps_ref[view, dim, tap]
        total = total + value
        matrix = jnp.where(distance == tap, value, matrix)
    return matrix / total


def hi_hi_lo(matrix, part):
    hi, lo = split(matrix)
    return jnp.where(part < 2, hi.astype(F32), lo.astype(F32)).astype(BF16)


def build_forward(taps_ref, wz_ref, wy_ref, wx_ref):
    def one(view, carry):
        col = iota((DEPTH, 3 * EDEPTH), 1)
        dist = col % EDEPTH - iota((DEPTH, 3 * EDEPTH), 0) - 1
        wz_ref[pl.ds(pl.multiple_of(view * DEPTH, DEPTH), DEPTH), :] = hi_hi_lo(
            spread_taps(dist, taps_ref, view, 0), col // EDEPTH
        )
        col = iota((ROWS, 3 * EROWS), 1)
        dist = col % EROWS - iota((ROWS, 3 * EROWS), 0) - 1
        wy_ref[view] = hi_hi_lo(spread_taps(dist, taps_ref, view, 1), col // EROWS)
        dist = iota((WIDTH, WIDTH), 0) - iota((WIDTH, WIDTH), 1) + HALF
        hi, lo = split(spread_taps(dist, taps_ref, view, 2))
        wx_ref[view, 0:WIDTH] = hi
        wx_ref[view, WIDTH : 2 * WIDTH] = hi
        wx_ref[view, 2 * WIDTH : 3 * WIDTH] = lo
        return carry

    lax.fori_loop(0, VIEWS, one, 0)


def build_backward(taps_ref, wz_ref, wy_ref, wx_ref, wide_ref):
    wide_ref[...] = jnp.zeros_like(wide_ref)

    def one(view, carry):
        shape = wide_ref.shape[1:]
        inner = iota(shape, 1) % (CHUNK * DEPTH) - view % CHUNK * DEPTH
        dist = iota(shape, 0) - inner - 1
        dist = jnp.where((inner >= 0) & (inner < DEPTH), dist, -1)
        wide_ref[view // CHUNK] += spread_taps(dist, taps_ref, view, 0)
        col = iota((EROWS, 3 * ROWS), 1)
        dist = iota((EROWS, 3 * ROWS), 0) - col % ROWS - 1
        wy_ref[view] = hi_hi_lo(spread_taps(dist, taps_ref, view, 1), col // ROWS)
        dist = iota((WIDTH, WIDTH), 1) - iota((WIDTH, WIDTH), 0) + HALF
        hi, lo = split(spread_taps(dist, taps_ref, view, 2))
        wx_ref[view, 0:WIDTH] = hi
        wx_ref[view, WIDTH : 2 * WIDTH] = hi
        wx_ref[view, 2 * WIDTH : 3 * WIDTH] = lo
        return carry

    lax.fori_loop(0, VIEWS, one, 0)
    wz_ref[...] = hi_hi_lo(wide_ref[...], iota(wide_ref.shape, 2) // (CHUNK * DEPTH))


def stacked(x, axis):
    hi, lo = split(x)
    return jnp.concatenate([hi, lo, hi], axis=axis)


def dot(a, b):
    return jnp.dot(a, b, preferred_element_type=F32)


def axial_forward(ext_ref, wz_ref, axial_ref):
    def one(step, carry):
        for inner in range(2):
            y = step * 4 + inner * 2
            field = jnp.concatenate(
                [ext_ref[pl.ds(y + k, EDEPTH, stride=EROWS), :] for k in range(2)], axis=1
            )
            out = dot(wz_ref[...], stacked(field, 0))
            for k in range(2):
                axial_ref[pl.ds(y + k, VIEWS * DEPTH, stride=EROWS), :] = out[
                    :, k * WIDTH : (k + 1) * WIDTH
                ]
        return carry

    lax.fori_loop(0, EROWS // 4, one, 0)


def lateral_forward(view, axial_ref, wy_ref, side_ref):
    for z in range(0, DEPTH, 2):
        base = (view * DEPTH + z) * EROWS
        field = jnp.concatenate(
            [
                axial_ref[pl.ds(pl.multiple_of(base + k * EROWS, EROWS), EROWS), :]
                for k in range(2)
            ],
            axis=1,
        )
        out = dot(wy_ref[view], stacked(field, 0))
        for k in range(2):
            side_ref[(z + k) * ROWS : (z + k + 1) * ROWS, :] = out[
                :, k * WIDTH : (k + 1) * WIDTH
            ]


def lateral_backward(view, side_ref, wy_ref, back_ref):
    for z in range(0, DEPTH, 2):
        field = jnp.concatenate(
            [side_ref[(z + k) * ROWS : (z + k + 1) * ROWS, :] for k in range(2)], axis=1
        )
        out = dot(wy_ref[view], stacked(field, 0))
        base = (view * DEPTH + z) * EROWS
        for k in range(2):
            back_ref[pl.ds(pl.multiple_of(base + k * EROWS, EROWS), EROWS), :] = out[
                :, k * WIDTH : (k + 1) * WIDTH
            ]


def axial_backward(c, edges, back_ref, wz_ref, out_ref):
    half = ROWS // 2

    def one(step, carry):
        for inner in range(2):
            spot = step * 4 + inner * 2
            y = spot + (jnp.where(step >= half // 4, ROWS, 0) if edges else PAD)
            field = jnp.concatenate(
                [
                    back_ref[pl.ds(c * CHUNK * SLAB + y + k, CHUNK * DEPTH, stride=EROWS), :]
                    for k in range(2)
                ],
                axis=1,
            )
            out = dot(wz_ref[c], stacked(field, 0))
            for k in range(2):
                place = pl.ds(spot + k, EDEPTH, stride=ROWS)
                part = out[:, k * WIDTH : (k + 1) * WIDTH]
                out_ref[place, :] = part if c == 0 else out_ref[place, :] + part
        return carry

    lax.fori_loop(0, ROWS // 4, one, 0)


CHUNK = 3
CHUNKS = VIEWS // CHUNK
CELLS = DEPTH * ROWS
SLAB = DEPTH * EROWS
EDGE = HALF * EROWS
BAND = HALF * ROWS
ANY = pl.BlockSpec(memory_space=pl.ANY)
VMEM = pl.BlockSpec(memory_space=pltpu.VMEM)
SMEM = pl.BlockSpec(memory_space=pltpu.SMEM)


def kernel(
    bricks, stacks, taps_ref, flags_ref, est_hbm, view_ref, out_ref, est_ref,
    mid0, mid1, stage, owned,
    halo, ext, wz, wy, wx, axial, side, blur,
    bz, by, bx, wide, back, spill_edges, spill_middle, from_edges, from_middle, to_brick, from_brick,
    send1, recv1, local1, send2, recv2, hsend, hrecv, ssend, srecv, tsend, trecv, usend, urecv, msend, mrecv, esem,
):
    mids = (mid0, mid1)
    me = lax.axis_index("brick")
    level = lax.axis_index("stack")
    part = CELLS // bricks

    def to(axis, index, source, target, send_sem, recv_sem):
        return pltpu.make_async_remote_copy(
            src_ref=source,
            dst_ref=target,
            send_sem=send_sem,
            recv_sem=recv_sem,
            device_id={axis: index},
            device_id_type=pl.DeviceIdType.MESH,
        )

    def peer(step):
        turn = lax.rem(step - 1 + lax.rem(level, 2) * (bricks // 2 - 1), bricks - 1)
        return lax.rem(me + 1 + turn, bricks)

    def rows(index):
        return pl.ds(pl.multiple_of(index * part, part), part)

    sides = (
        ("brick", me > 0, me - 1, 0),
        ("brick", me < bricks - 1, me + 1, 1),
    )
    floors = (
        ("stack", level > 0, level - 1, 0),
        ("stack", level < stacks - 1, level + 1, 1),
    )

    load = pltpu.make_async_copy(est_hbm, est_ref, esem.at[0])
    load.start()
    barrier = pltpu.get_barrier_semaphore()

    def greet(step, carry):
        pl.semaphore_signal(
            barrier, inc=1, device_id={"brick": peer(step)}, device_id_type=pl.DeviceIdType.MESH
        )
        return carry

    lax.fori_loop(1, bricks, greet, 0)
    for axis, there, index, _ in floors:
        @pl.when(there)
        def _():
            pl.semaphore_signal(
                barrier, inc=1, device_id={axis: index}, device_id_type=pl.DeviceIdType.MESH
            )
    pl.semaphore_wait(
        barrier,
        bricks - 1 + jnp.minimum(level, 1) + jnp.minimum(stacks - 1 - level, 1),
    )

    def halo_copy(index, up):
        source = est_hbm.at[:, pl.ds(ROWS - PAD if up else 0, PAD), :]
        return to("brick", index, source, halo.at[1 - up], hsend.at[up], hrecv.at[1 - up])

    for _, there, index, up in sides:
        @pl.when(there)
        def _():
            halo_copy(index, up).start()

    def first(step, c):
        to_index = peer(step)
        return to(
            "brick",
            to_index,
            view_ref.at[pl.ds(c * CHUNK, CHUNK), rows(to_index), :],
            mids[c].at[me],
            send1.at[c, to_index],
            recv1.at[c, me],
        )

    def first_in(step, c):
        source = peer(step)
        return to(
            "brick", source, mids[c].at[source], mids[c].at[source],
            send1.at[c, source], recv1.at[c, source],
        )

    def own(c):
        return pltpu.make_async_copy(
            view_ref.at[pl.ds(c * CHUNK, CHUNK), rows(me), :], mids[c].at[me], local1.at[c]
        )

    def second(step, c):
        to_index = peer(step)
        return to(
            "brick",
            to_index,
            stage.at[to_index, pl.ds(c * CHUNK, CHUNK)],
            owned.at[pl.ds(c * CHUNK, CHUNK), rows(me), :],
            send2.at[c, to_index],
            recv2.at[c, me],
        )

    def second_in(step, c):
        source = peer(step)
        target = owned.at[pl.ds(c * CHUNK, CHUNK), rows(source), :]
        return to("brick", source, target, target, send2.at[c, source], recv2.at[c, source])

    def each(make, act, c):
        def body(step, carry):
            act(make(step, c))
            return carry

        lax.fori_loop(1, bricks, body, 0)

    for c in range(CHUNKS):
        own(c).start()
        each(first, lambda copy: copy.start(), c)

    build_forward(taps_ref, wz, wy, wx)

    for z in (0, EDEPTH - 1):
        ext[z * EROWS : (z + 1) * EROWS, :] = jnp.zeros((EROWS, WIDTH), F32)
    for _, there, _, up in floors:
        @pl.when(jnp.logical_not(there))
        def _():
            start = (PAD + DEPTH) * EROWS if up else EROWS
            ext[start : start + EDGE, :] = jnp.zeros((EDGE, WIDTH), F32)
    for _, there, index, up in sides:
        @pl.when(there)
        def _():
            to(
                "brick", index, halo.at[up], halo.at[up], hsend.at[up], hrecv.at[up]
            ).wait_recv()

        @pl.when(jnp.logical_not(there))
        def _():
            halo[up] = jnp.zeros((DEPTH, PAD, WIDTH), F32)
    load.wait()
    for z in range(DEPTH):
        base = (PAD + z) * EROWS
        ext[base : base + PAD, :] = halo[0, z]
        ext[base + PAD : base + PAD + ROWS, :] = est_ref[z]
        ext[base + PAD + ROWS : base + EROWS, :] = halo[1, z]

    def slab_copy(index, up):
        start = (PAD + 1 if up else PAD) * EROWS
        target = EROWS if up else (PAD + DEPTH) * EROWS
        return to(
            "stack", index, ext.at[pl.ds(start, EDGE), :], ext.at[pl.ds(target, EDGE), :],
            ssend.at[up], srecv.at[1 - up],
        )

    for _, there, index, up in floors:
        @pl.when(there)
        def _():
            slab_copy(index, up).start()
    build_backward(taps_ref, bz, by, bx, wide)
    for _, there, index, up in floors:
        @pl.when(there)
        def _():
            start = (PAD + DEPTH) * EROWS if up else EROWS
            target = ext.at[pl.ds(start, EDGE), :]
            to("stack", index, target, target, ssend.at[up], srecv.at[up]).wait_recv()
    axial_forward(ext, wz, axial)

    for c in range(CHUNKS):
        own(c).wait()
        each(first_in, lambda copy: copy.wait_recv(), c)

        def pick(target, carry, c=c):
            for k in range(CHUNK):
                view = c * CHUNK + k
                source = lax.rem(target + bricks - flags_ref[view], bricks)
                stage[target, view] = mids[c][source, k]
            return carry

        lax.fori_loop(0, bricks, pick, 0)
        each(second, lambda copy: copy.start(), c)
        for k in range(CHUNK):
            view = c * CHUNK + k
            owned[view, rows(me), :] = stage[me, view]

        def one(view, carry):
            lateral_forward(view, axial, wy, side)
            blur[view] = dot(stacked(side[...], 1), wx[view])
            return carry

        lax.fori_loop(c * CHUNK, (c + 1) * CHUNK, one, 0)

    for c in range(CHUNKS):
        each(second_in, lambda copy: copy.wait_recv(), c)

        def one(view, carry):
            cover = flags_ref[VIEWS + view].astype(F32)
            ratio = cover * owned[view] / blur[view]
            side[...] = dot(stacked(ratio, 1), bx[view])
            lateral_backward(view, side, by, back)
            return carry

        lax.fori_loop(c * CHUNK, (c + 1) * CHUNK, one, 0)
        if c < CHUNKS - 1:
            axial_backward(c, True, back, bz, spill_edges)
            axial_backward(c, False, back, bz, spill_middle)

    def spill_copy(index, up, source, target, send_sem, recv_sem):
        start = (PAD + DEPTH) * ROWS if up else ROWS
        return to(
            "stack", index, source.at[pl.ds(start, BAND), :], target.at[1 - up],
            send_sem.at[up], recv_sem.at[1 - up],
        )

    spills = (
        (True, spill_edges, from_edges, tsend, trecv),
        (False, spill_middle, from_middle, msend, mrecv),
    )
    for edges, source, target, send_sem, recv_sem in spills:
        axial_backward(CHUNKS - 1, edges, back, bz, source)
        for _, there, index, up in floors:
            @pl.when(there)
            def _():
                spill_copy(index, up, source, target, send_sem, recv_sem).start()

    def take(source, target, send_sem, recv_sem):
        for _, there, index, up in floors:
            @pl.when(there)
            def _():
                to(
                    "stack", index, target.at[up], target.at[up], send_sem.at[up], recv_sem.at[up]
                ).wait_recv()
                start = (PAD + 1 if up else PAD) * ROWS
                source[start : start + BAND, :] += target[up]

    take(*spills[0][1:])
    for z in range(DEPTH):
        base = (PAD + z) * ROWS
        to_brick[0, z] = spill_edges[base : base + PAD, :]
        to_brick[1, z] = spill_edges[base + ROWS - PAD : base + ROWS, :]

    def side_copy(index, up):
        return to(
            "brick", index, to_brick.at[up], from_brick.at[1 - up], usend.at[up], urecv.at[1 - up]
        )

    for _, there, index, up in sides:
        @pl.when(there)
        def _():
            side_copy(index, up).start()
    count = jnp.float32(0.0)
    for view in range(VIEWS):
        count = count + flags_ref[VIEWS + view].astype(F32)

    for c in range(CHUNKS):
        each(first, lambda copy: copy.wait_send(), c)
        each(second, lambda copy: copy.wait_send(), c)
    for _, there, index, up in sides:
        @pl.when(there)
        def _():
            halo_copy(index, up).wait_send()
    for _, there, index, up in floors:
        @pl.when(there)
        def _():
            slab_copy(index, up).wait_send()
    take(*spills[1][1:])
    for _, there, index, up in floors:
        @pl.when(there)
        def _():
            for _, source, target, send_sem, recv_sem in spills:
                spill_copy(index, up, source, target, send_sem, recv_sem).wait_send()
    for _, there, index, up in sides:
        @pl.when(there)
        def _():
            to(
                "brick", index, from_brick.at[up], from_brick.at[up], usend.at[up], urecv.at[up]
            ).wait_recv()
            side_copy(index, up).wait_send()

        @pl.when(jnp.logical_not(there))
        def _():
            from_brick[up] = jnp.zeros((DEPTH, PAD, WIDTH), F32)
    for z in range(DEPTH):
        base = (PAD + z) * ROWS
        half = ROWS - PAD
        low = spill_middle[base : base + half, :] + from_brick[0, z]
        high = spill_middle[base + half : base + ROWS, :] + from_brick[1, z]
        out_ref[z, 0:half, :] = est_ref[z, 0:half, :] * low / count
        out_ref[z, half:ROWS, :] = est_ref[z, half:ROWS, :] * high / count


def shards(estimate, view_data, psf_taps, offsets, coverage):
    bricks = lax.axis_size("brick")
    stacks = lax.axis_size("stack")
    part = CELLS // bricks
    vmem = lambda *shape: pltpu.VMEM(shape, F32)
    half = lambda *shape: pltpu.VMEM(shape, BF16)
    sems = lambda *shape: pltpu.SemaphoreType.DMA(shape)
    scratch = [vmem(*estimate.shape)] + [vmem(bricks, CHUNK, part, WIDTH)] * CHUNKS
    scratch += [
        vmem(bricks, VIEWS, part, WIDTH),
        vmem(VIEWS, CELLS, WIDTH),
        vmem(2, DEPTH, PAD, WIDTH),
        vmem(EDEPTH * EROWS, WIDTH),
        half(VIEWS * DEPTH, 3 * EDEPTH),
        half(VIEWS, ROWS, 3 * EROWS),
        half(VIEWS, 3 * WIDTH, WIDTH),
        vmem(VIEWS * SLAB, WIDTH),
        vmem(CELLS, WIDTH),
        vmem(VIEWS, CELLS, WIDTH),
        half(CHUNKS, EDEPTH, 3 * CHUNK * DEPTH),
        half(VIEWS, EROWS, 3 * ROWS),
        half(VIEWS, 3 * WIDTH, WIDTH),
        vmem(CHUNKS, EDEPTH, 3 * CHUNK * DEPTH),
        vmem(VIEWS * SLAB, WIDTH),
        vmem(EDEPTH * ROWS, WIDTH),
        vmem(EDEPTH * ROWS, WIDTH),
        vmem(2, BAND, WIDTH),
        vmem(2, BAND, WIDTH),
        vmem(2, DEPTH, PAD, WIDTH),
        vmem(2, DEPTH, PAD, WIDTH),
        sems(CHUNKS, bricks),
        sems(CHUNKS, bricks),
        sems(CHUNKS),
        sems(CHUNKS, bricks),
        sems(CHUNKS, bricks),
    ]
    scratch += [sems(2)] * 10 + [sems(1)]
    return pl.pallas_call(
        functools.partial(kernel, bricks, stacks),
        out_shape=jax.ShapeDtypeStruct(estimate.shape, F32),
        in_specs=[SMEM, SMEM, ANY, ANY],
        out_specs=VMEM,
        scratch_shapes=scratch,
        compiler_params=pltpu.CompilerParams(
            collective_id=0, has_side_effects=True, vmem_limit_bytes=48 * 1024 * 1024
        ),
    )(
        psf_taps, jnp.concatenate([offsets, coverage[:, 0]]), estimate,
        view_data.reshape(VIEWS, CELLS, WIDTH),
    )


def solution(mesh):
    placed = (
        P("stack", "brick", None),
        P(None, "stack", "brick", None),
        P(),
        P(),
        P(None, "brick"),
    )
    return jax.shard_map(
        shards, mesh=mesh, in_specs=placed, out_specs=P("stack", "brick", None), check_vma=False
    )
```
